256 devices in a mesh: row: 16 (over x, z_lo), col: 16 (over y, z_hi, core).
Axes of the slice: x: 4, y: 4, z: 8 (z_hi: 2, z_lo: 4; z = z_hi * 4 + z_lo), core: 2. Of those that a mesh axis runs over, the one named last changes fastest.
Arguments:
- query_proj: bfloat16 [128, 256, 768], P('row', 'col'), may hold values from -1 to 1
- key_proj: bfloat16 [128, 256, 768], P('row', 'col'), may hold values from -1 to 1
- value_proj: bfloat16 [128, 256, 768], P('row', 'col'), may hold values from -0.77734375 to 0.77734375
- grad_output: bfloat16 [128, 256, 768], P('row', 'col'), may hold values from -120 to 120
- log_totals: float32 [12, 256], P(None, 'col'), may hold values from 6 to 7.5
Outputs:
- grad_query: bfloat16 [128, 256, 768], P('row', 'col')
- grad_key: bfloat16 [128, 256, 768], P('row', 'col')
- grad_value: bfloat16 [128, 256, 768], P('row', 'col')
The draws below stay inside these ranges and needn't reach their ends.
All inputs are finite; a program needn't handle non-finite values.
Results may differ from the reference program's by a relative error of at most 0.011.
Values may be sent and summed in bfloat16 or wider, within the bound.
A program may use at most 128 MiB of HBM per device.

```python
import jax
import jax.numpy as jnp

H = 12
E = 64
HE = 768
R = 128
C = 256


def draw_query_proj(key, part):
    key = jax.random.fold_in(key, 11)
    spread = 0.894 * float(R * E) ** (-0.25)
    normal_key = jax.random.fold_in(key, 0)
    values = jax.random.normal(normal_key, (R, C, H * E), jnp.float32)
    return jnp.clip(values * spread, -1.0, 1.0).astype(jnp.bfloat16)


def draw_key_proj(key, part):
    key = jax.random.fold_in(key, 13)
    spread = 0.894 * float(R * E) ** (-0.25)
    normal_key = jax.random.fold_in(key, 0)
    values = jax.random.normal(normal_key, (R, C, H * E), jnp.float32)
    return jnp.clip(values * spread, -1.0, 1.0).astype(jnp.bfloat16)


def level_of(own_key, shape, cuts, least, high):
    def one(position, shards_of):
        steps = jax.random.uniform(jax.random.fold_in(jax.random.fold_in(own_key, 6), position), (shards_of,), jnp.float32, least / len(cuts), high / len(cuts))
        return jnp.repeat(jnp.exp(steps), shape[position] // shards_of).reshape((-1,) + (1,) * (len(shape) - position - 1))

    loudness = one(*cuts[0])
    for cut in cuts[1:]:
        loudness = loudness * one(*cut)
    return loudness


def normal_values(rng, extent, scale, most, pieces=(), dtype=jnp.bfloat16):
    level = level_of(rng, extent, pieces, -0.22, 0.18) if pieces else 1.0
    entries = jax.random.normal(rng, extent, jnp.float32) * scale * level
    return jnp.minimum(jnp.maximum(entries, -most), most).astype(dtype)


def setup_inputs(seed: int = 0) -> dict:
    arg_keys = jax.random.split(jax.random.key(seed), 6)
    return {
        "query_proj": draw_query_proj(jax.random.fold_in(arg_keys[5], 71), 0),
        "key_proj": draw_key_proj(jax.random.fold_in(arg_keys[5], 71), 0),
        "value_proj": normal_values(arg_keys[2], (R, C, HE), 0.13, 0.77734375, ((0, 16), (1, 16))),
        "grad_output": normal_values(arg_keys[3], (R, C, HE), 20.0, 120.0, ((0, 16), (1, 16))),
        "log_totals": jnp.clip(6.0 + 1.5 * jax.random.uniform(arg_keys[4], (H, C), jnp.float32) ** level_of(arg_keys[4], (H, C), ((1, 16),), -0.2, 0.2), 6.0, 7.5),
    }


def reference(query_proj, key_proj, value_proj, grad_output, log_totals):
    query_heads = query_proj.astype(jnp.float32).reshape(R, C, H, E)
    key_heads = key_proj.astype(jnp.float32).reshape(R, C, H, E)
    value_heads = value_proj.astype(jnp.float32).reshape(R, C, H, E)
    output_heads = grad_output.astype(jnp.float32).reshape(R, C, H, E)
    logits = jnp.einsum("rihe,rjhe->hij", query_heads, key_heads)
    probs = jnp.exp(logits - log_totals[:, :, None])
    grad_probs = jnp.einsum("rihe,rjhe->hij", output_heads, value_heads)
    delta = jnp.sum(probs * grad_probs, axis=2, keepdims=True)
    weights = probs.astype(jnp.bfloat16)
    grad_logits = (probs * (grad_probs - delta)).astype(jnp.bfloat16)
    logit_grads = grad_logits.astype(jnp.float32)
    grad_query = jnp.einsum("hij,rjhe->rihe", logit_grads, key_heads).reshape(R, C, H * E)
    grad_key = jnp.einsum("hij,rihe->rjhe", logit_grads, query_heads).reshape(R, C, H * E)
    grad_value = jnp.einsum("hij,rihe->rjhe", weights.astype(jnp.float32), output_heads).reshape(R, C, H * E)
    return (grad_query.astype(jnp.bfloat16), grad_key.astype(jnp.bfloat16), grad_value.astype(jnp.bfloat16))
```

```python
import jax
import jax.numpy as jnp
from jax import lax
from jax.experimental import pallas as pl
from jax.experimental.pallas import tpu as pltpu
from jax.sharding import PartitionSpec as P

MESH = pl.DeviceIdType.MESH
NX, NY, NZL, NZH, NC = 4, 4, 4, 2, 2
CH = 3
F32, BF16 = jnp.float32, jnp.bfloat16

ORDER = (
    ("in", 0), ("in", 1), ("in", 2),
    ("A", 0), ("B", 0), ("C", 0), ("A", 1), ("B", 1), ("D", 0), ("C", 1), ("E", 0),
    ("A", 2), ("k", 0), ("k", 1), ("k", 2), ("B", 2), ("F", 0), ("D", 1), ("C", 2), ("E", 1), ("F", 1), ("D", 2),
    ("G", 0), ("G", 1), ("E", 2), ("F", 2), ("G", 2), ("H", 0), ("H", 1), ("H", 2),
)


def swap_halves(low, high):
    lane = lax.broadcasted_iota(jnp.int32, low.shape, low.ndim - 1)
    first = jnp.concatenate([low[..., :64], high[..., :64]], axis=-1)
    second = jnp.concatenate([low[..., 64:], high[..., 64:]], axis=-1)
    del lane
    return first, second


def kernel(
    q_ref, k_ref, v_ref, g_ref, l_ref, dq_ref, dk_ref, dv_ref,
    st, rc, tt, c1, uu, x1, ww, z1, ag, oo, orr, lsend, lrecv,
    in_s, in_r, core_s, core_r, x_s, x_r, z_s, z_r, ga_s, ga_r, out_s, out_r, l_s, l_r,
):
    row, col = lax.axis_index("row"), lax.axis_index("col")
    x, zl = row // NZL, row % NZL
    y, zh, c = col // 4, (col // 2) % 2, col % 2
    here = y * 2 + c

    def dev(x, zl, y, zh, c):
        return (x * NZL + zl, (y * 2 + zh) * 2 + c)

    def send(src, dst, ssem, rsem, target):
        pltpu.make_async_remote_copy(
            src, dst, ssem, rsem, device_id=target, device_id_type=MESH
        ).start()

    def wait(ref, sem):
        pltpu.make_async_copy(ref, ref, sem).wait()

    def rot(value, step, count):
        return lax.rem(value + step, count)

    near = [(dy, dc) for dy in range(NY) for dc in range(NC)]

    l_to = dev(y, 2 * c + zl % 2, rot(x, 1, 4), zl // 2, zh)
    l_from = dev(rot(y, 3, 4), zh * 2 + zl % 2, x, c, zl // 2)

    barrier = pltpu.get_barrier_semaphore()
    peers = [dev(x, zl, rot(y, dy, 4), zh, rot(c, dc, 2)) for dy, dc in near[1:]]
    peers += [dev(x, zl, rot(y, dy, 4), 1 - zh, rot(c, dc, 2)) for dy, dc in near]
    peers += [dev(rot(x, d, 4), zl, y, zh, c) for d in range(1, 4)]
    peers += [dev(x, rot(zl, d, 4), y, zh, c) for d in range(1, 4)]
    peers += [dev(x, rot(zl, d, 4), y, 1 - zh, c) for d in range(1, 4)]
    peers += [l_from]
    for peer in peers:
        pl.semaphore_signal(barrier, inc=1, device_id=peer, device_id_type=MESH)

    def pack(ch):
        for a, ref in enumerate((q_ref, g_ref, k_ref, v_ref)):
            for yy in range(NY):
                head = yy * CH + ch
                tile = head // 2
                part = ref[:, :, tile * 128 : tile * 128 + 128].reshape(4, 2, 16, 128)
                block = swap_halves(part[:, 0], part[:, 1])[head % 2]
                for cc in range(NC):
                    st[ch, yy * 2 + cc, a] = block[2 * cc : 2 * cc + 2]

    sub = lax.broadcasted_iota(jnp.int32, (8, 16), 0) + 8 * (zl % 2)
    lane = lax.broadcasted_iota(jnp.int32, (8, 16), 1)
    for ch in range(CH):
        line = l_ref[pl.ds(rot(x, 1, 4) * CH + ch, 1), :]
        column = jnp.sum(jnp.where(sub == lane, line, 0.0), axis=1, keepdims=True)
        lsend[ch] = jnp.broadcast_to(column, (8, 128))

    pack(0)
    pl.semaphore_wait(barrier, len(peers))
    send(lsend, lrecv, l_s, l_r, l_to)

    def step_in(ch):
        if ch:
            pack(ch)
        for dy, dc in near:
            yy, cc = rot(y, dy, 4), rot(c, dc, 2)
            send(
                st.at[ch, yy * 2 + cc, pl.ds(0, 2)], rc.at[ch, zh, here, pl.ds(0, 2)],
                in_s.at[ch, 0], in_r.at[ch, 0], dev(x, zl, yy, 1 - zh, cc),
            )
        for dy, dc in near[1:]:
            yy, cc = rot(y, dy, 4), rot(c, dc, 2)
            send(
                st.at[ch, yy * 2 + cc], rc.at[ch, zh, here],
                in_s.at[ch, 1], in_r.at[ch, 1], dev(x, zl, yy, zh, cc),
            )
        pltpu.make_async_copy(st.at[ch, here], rc.at[ch, zh, here], in_r.at[ch, 1]).start()

    def step_k(ch):
        for dy, dc in near:
            yy, cc = rot(y, dy, 4), rot(c, dc, 2)
            send(
                st.at[ch, yy * 2 + cc, pl.ds(2, 1)], rc.at[ch, zh, here, pl.ds(2, 1)],
                in_s.at[ch, 2], in_r.at[ch, 2], dev(x, zl, yy, 1 - zh, cc),
            )

    def both(ch, a):
        return jnp.concatenate(
            [rc[ch, :, :, a, rp].reshape(256, 128) for rp in range(2)], axis=1
        )

    def half(ch, side, a):
        return jnp.concatenate(
            [rc[ch, side, :, a, rp].reshape(128, 128) for rp in range(2)], axis=1
        )

    def step_a(ch):
        wait(rc.at[ch, 1 - zh, :, pl.ds(0, 2)], in_r.at[ch, 0])
        wait(rc.at[ch, zh], in_r.at[ch, 1])
        for n, (left, right) in enumerate(((0, 2), (1, 3))):
            part = lax.dot_general(
                both(ch, left), half(ch, zh, right), (((1,), (1,)), ((), ())),
                preferred_element_type=F32,
            )
            tt[ch, :, n] = part.reshape(32, 8, 128)
        send(
            tt.at[ch, pl.ds((1 - c) * 16, 16)], c1.at[ch], core_s.at[ch], core_r.at[ch],
            dev(x, zl, y, zh, 1 - c),
        )

    def step_b(ch):
        wait(c1.at[ch], core_r.at[ch])
        total = tt[ch, pl.ds(c * 16, 16)] + c1[ch]
        uu[ch] = total.reshape(4, 4, 2, 8, 128)
        for d in (2, 1, 3):
            to = rot(x, d, 4)
            send(uu.at[ch, to], x1.at[ch, d - 1], x_s.at[ch], x_r.at[ch], dev(to, zl, y, zh, c))

    def step_c(ch):
        wait(x1.at[ch], x_r.at[ch])
        ww[ch] = (uu[ch, x] + x1[ch, 0]) + (x1[ch, 1] + x1[ch, 2])
        for d in range(4):
            to = rot(zl, d, 4)
            send(
                ww.at[ch, to], z1.at[ch, 3 + d], z_s.at[ch], z_r.at[ch], dev(x, to, y, 1 - zh, c)
            )
        for d in range(1, 4):
            to = rot(zl, d, 4)
            send(ww.at[ch, to], z1.at[ch, d - 1], z_s.at[ch], z_r.at[ch], dev(x, to, y, zh, c))

    def step_d(ch):
        if ch == 0:
            wait(lrecv, l_r)
        wait(z1.at[ch], z_r.at[ch])
        own = (ww[ch, zl] + z1[ch, 0]) + (z1[ch, 1] + z1[ch, 2])
        other = (z1[ch, 3] + z1[ch, 4]) + (z1[ch, 5] + z1[ch, 6])
        logs = lrecv[ch]
        p_own = jnp.exp(own[0] - logs)
        p_other = jnp.exp(other[0] - logs)
        delta = jnp.sum(p_own * own[1] + p_other * other[1], axis=1, keepdims=True)
        d_own = p_own * (own[1] - delta)
        d_other = p_other * (other[1] - delta)
        ag[ch, c, x, zl, 0] = jnp.concatenate([p_own, d_own], axis=0).astype(BF16)
        ag[ch, c, x, zl, 1] = jnp.concatenate([d_other, d_other], axis=0).astype(BF16)
        block = ag.at[ch, c, x, zl]
        for d in range(1, 4):
            send(
                block, block, ga_s.at[ch, 0, d - 1], ga_r.at[ch, 0, d - 1],
                dev(x, rot(zl, d, 4), y, zh, c),
            )

    def step_e(ch):
        for d in range(1, 4):
            wait(ag.at[ch, c, x, rot(zl, 4 - d, 4)], ga_r.at[ch, 0, d - 1])
        block = ag.at[ch, c, x]
        for d in (2, 1, 3):
            send(
                block, block, ga_s.at[ch, 1, d - 1], ga_r.at[ch, 1, d - 1],
                dev(rot(x, d, 4), zl, y, zh, c),
            )

    def step_f(ch):
        for d in range(1, 4):
            wait(ag.at[ch, c, rot(x, 4 - d, 4)], ga_r.at[ch, 1, d - 1])
        block = ag.at[ch, c]
        send(block, block, ga_s.at[ch, 2, 0], ga_r.at[ch, 2, 0], dev(x, zl, y, zh, 1 - c))

    def step_g(ch):
        wait(ag.at[ch, 1 - c], ga_r.at[ch, 2, 0])
        wait(rc.at[ch, 1 - zh, :, pl.ds(2, 1)], in_r.at[ch, 2])
        first = ag[ch, :, :, :, 0].reshape(32, 16, 128).astype(F32)
        weights = first[:, :8].reshape(256, 128).astype(BF16)
        slopes = first[:, 8:].reshape(256, 128).astype(BF16)
        mine = ag[ch, zh].reshape(16, 2, 16, 128).astype(F32)
        own = mine[:, 0, 8:].reshape(128, 128).astype(BF16)
        other = mine[:, 1, :8].reshape(128, 128).astype(BF16)
        down = (((0,), (0,)), ((), ()))
        across = (((1,), (0,)), ((), ()))
        dq = lax.dot_general(own, half(ch, zh, 2), across, preferred_element_type=F32)
        dq += lax.dot_general(other, half(ch, 1 - zh, 2), across, preferred_element_type=F32)
        dk = lax.dot_general(slopes, both(ch, 0), down, preferred_element_type=F32)
        dv = lax.dot_general(weights, both(ch, 1), down, preferred_element_type=F32)
        for a, value in enumerate((dq, dk, dv)):
            for rp in range(2):
                piece = value[:, rp * 128 : rp * 128 + 128].astype(BF16)
                oo[ch, :, a, rp] = piece.reshape(8, 16, 128)
        for dy, dc in near[1:]:
            yy, cc = rot(y, dy, 4), rot(c, dc, 2)
            send(
                oo.at[ch, yy * 2 + cc], orr.at[ch, here], out_s.at[ch], out_r.at[ch],
                dev(x, zl, yy, zh, cc),
            )
        pltpu.make_async_copy(oo.at[ch, here], orr.at[ch, here], out_r.at[ch]).start()

    def step_h(ch):
        wait(orr.at[ch], out_r.at[ch])

    steps = {
        "in": step_in, "k": step_k, "A": step_a, "B": step_b, "C": step_c, "D": step_d,
        "E": step_e, "F": step_f, "G": step_g, "H": step_h,
    }
    for name, ch in ORDER:
        steps[name](ch)

    for a, ref in enumerate((dq_ref, dk_ref, dv_ref)):
        for tile in range(6):
            pair = []
            for head in (2 * tile, 2 * tile + 1):
                yy, ch = head // CH, head % CH
                pair.append(orr[ch, pl.ds(yy * 2, 2), a].reshape(4, 16, 128))
            first, second = swap_halves(*pair)
            lanes = pl.ds(tile * 128, 128)
            for n in range(4):
                ref[2 * n, :, lanes] = first[n]
                ref[2 * n + 1, :, lanes] = second[n]

    wait(lsend, l_s)
    for ch in range(CH):
        wait(st.at[ch, :, pl.ds(0, 2)], in_s.at[ch, 0])
        wait(st.at[ch, pl.ds(0, 7)], in_s.at[ch, 1])
        wait(st.at[ch, :, pl.ds(2, 1)], in_s.at[ch, 2])
        wait(c1.at[ch], core_s.at[ch])
        wait(x1.at[ch], x_s.at[ch])
        wait(z1.at[ch], z_s.at[ch])
        for d in range(3):
            wait(ag.at[ch, c, x, zl], ga_s.at[ch, 0, d])
            wait(ag.at[ch, c, x], ga_s.at[ch, 1, d])
        wait(ag.at[ch, c], ga_s.at[ch, 2, 0])
        wait(oo.at[ch, pl.ds(0, 7)], out_s.at[ch])


def body(query_proj, key_proj, value_proj, grad_output, log_totals):
    dma = pltpu.SemaphoreType.DMA
    vmem = pl.BlockSpec(memory_space=pltpu.VMEM)
    return pl.pallas_call(
        kernel,
        out_shape=[jax.ShapeDtypeStruct(query_proj.shape, BF16)] * 3,
        in_specs=[vmem] * 5,
        out_specs=[vmem] * 3,
        scratch_shapes=[
            pltpu.VMEM((CH, 8, 4, 2, 16, 128), BF16),
            pltpu.VMEM((CH, 2, 8, 4, 2, 16, 128), BF16),
            pltpu.VMEM((CH, 32, 2, 8, 128), F32),
            pltpu.VMEM((CH, 16, 2, 8, 128), F32),
            pltpu.VMEM((CH, 4, 4, 2, 8, 128), F32),
            pltpu.VMEM((CH, 3, 4, 2, 8, 128), F32),
            pltpu.VMEM((CH, 4, 2, 8, 128), F32),
            pltpu.VMEM((CH, 7, 2, 8, 128), F32),
            pltpu.VMEM((CH, 2, 4, 4, 2, 16, 128), BF16),
            pltpu.VMEM((CH, 8, 3, 2, 16, 128), BF16),
            pltpu.VMEM((CH, 8, 3, 2, 16, 128), BF16),
            pltpu.VMEM((CH, 8, 128), F32),
            pltpu.VMEM((CH, 8, 128), F32),
            dma((CH, 3)), dma((CH, 3)),
            dma((CH,)), dma((CH,)),
            dma((CH,)), dma((CH,)),
            dma((CH,)), dma((CH,)),
            dma((CH, 3, 3)), dma((CH, 3, 3)),
            dma((CH,)), dma((CH,)),
            dma, dma,
        ],
        compiler_params=pltpu.CompilerParams(
            collective_id=0, has_side_effects=True, vmem_limit_bytes=40 * 2**20
        ),
        name="tied_row_backward",
    )(query_proj, key_proj, value_proj, grad_output, log_totals)


def solution(mesh):
    in_specs = (
        P("row", "col", None),
        P("row", "col", None),
        P("row", "col", None),
        P("row", "col", None),
        P(None, "col"),
    )
    out_specs = (P("row", "col", None), P("row", "col", None), P("row", "col", None))
    return jax.shard_map(body, mesh=mesh, in_specs=in_specs, out_specs=out_specs, check_vma=False)
```

```python
import jax
import jax.numpy as jnp
from jax import lax
from jax.experimental import pallas as pl
from jax.experimental.pallas import tpu as pltpu
from jax.sharding import PartitionSpec as P

MESH = pl.DeviceIdType.MESH
NY, NC = 4, 2
CH = 3
F32, BF16 = jnp.float32, jnp.bfloat16
Q, K, G, V = 0, 1, 2, 3
S, D = 0, 1

ORDER = (
    "I0", "L0", "I1", "I2", "J0", "J1", "J2", "As0", "Bs0", "As1", "Bs1", "As2", "Bs2", "Cs0",
    "Cs1", "Cs2", "K0", "K1", "Ad0", "Bd0", "Ad1", "Bd1", "Cd0", "Ad2", "Bd2", "Cd1", "Cd2", "Ds0",
    "Ds1", "Ds2", "Dp0", "Dd0", "Dd1", "Dd2", "K2", "Ep0", "Ed0", "Ed1", "Ed2", "Fp0", "Fd0", "Fd1",
    "Fd2", "Gp0", "Gp1", "Gp2", "Gd0", "Gd1", "Gd2", "Hp0", "Hd0",
)


def swap_halves(low, high):
    first = jnp.concatenate([low[..., :64], high[..., :64]], axis=-1)
    second = jnp.concatenate([low[..., 64:], high[..., 64:]], axis=-1)
    return first, second


def kernel(
    q_hbm, k_hbm, v_hbm, g_hbm, l_hbm, dq_hbm, dk_hbm, dv_hbm,
    q_ref, k_ref, v_ref, g_ref, l_ref, dq_ref, dk_ref, dv_ref, load_s, store_s,
    st, rc, tt, c1, uu, x1, ww, z1, pp, agp, psend, agd, dsend, oo, orr, lsend, lrecv,
    in_s, in_r, core_s, core_r, x_s, x_r, z_s, z_r, gp_s, gp_r, gd_s, gd_r, out_s, out_r, l_s, l_r,
):
    row, col = lax.axis_index("row"), lax.axis_index("col")
    x, zl = row // 4, row % 4
    y, zh, c = col // 4, (col // 2) % 2, col % 2
    here = y * 2 + c

    def dev(x, zl, y, zh, c):
        return (x * 4 + zl, (y * 2 + zh) * 2 + c)

    def send(src, dst, ssem, rsem, target):
        pltpu.make_async_remote_copy(
            src, dst, ssem, rsem, device_id=target, device_id_type=MESH
        ).start()

    def wait(ref, sem):
        pltpu.make_async_copy(ref, ref, sem).wait()

    def rot(value, step, count):
        return lax.rem(value + step, count)

    loads = [
        pltpu.make_async_copy(src, dst, load_s.at[n])
        for n, (src, dst) in enumerate((
            (q_hbm, q_ref), (k_hbm, k_ref), (g_hbm, g_ref), (v_hbm, v_ref), (l_hbm, l_ref)
        ))
    ]
    for load in loads:
        load.start()

    near = [(dy, dc) for dy in range(NY) for dc in range(NC)]
    core_peer = dev(x, zl, y, zh, 1 - c)

    def along(step):
        z = rot(zh * 4 + zl, step, 8)
        return z % 4, z // 4

    l_to = dev(y, 2 * c + zl % 2, rot(x, 1, 4), zl // 2, zh)
    l_from = dev(rot(y, 3, 4), zh * 2 + zl % 2, x, c, zl // 2)

    barrier = pltpu.get_barrier_semaphore()
    peers = [dev(x, zl, rot(y, dy, 4), zh, rot(c, dc, 2)) for dy, dc in near[1:]]
    peers += [dev(x, zl, rot(y, dy, 4), 1 - zh, rot(c, dc, 2)) for dy, dc in near]
    peers += [dev(rot(x, d, 4), zl, y, zh, c) for d in range(1, 4)]
    peers += [dev(x, rot(zl, d, 4), y, zh, c) for d in range(1, 4)]
    peers += [dev(x, rot(zl, d, 4), y, 1 - zh, c) for d in range(1, 4)]
    peers += [l_from]
    for peer in peers:
        pl.semaphore_signal(barrier, inc=1, device_id=peer, device_id_type=MESH)

    def pack(ch, arrays):
        for a, ref in arrays:
            for yy in range(NY):
                head = yy * CH + ch
                tile = head // 2
                part = ref[:, :, tile * 128 : tile * 128 + 128].reshape(4, 2, 16, 128)
                block = swap_halves(part[:, 0], part[:, 1])[head % 2]
                for cc in range(NC):
                    st[ch, yy * 2 + cc, a] = block[2 * cc : 2 * cc + 2]

    loads[0].wait()
    loads[1].wait()
    pack(0, ((Q, q_ref), (K, k_ref)))
    pl.semaphore_wait(barrier, len(peers))

    def cross(ch, a, n):
        for dy, dc in near:
            yy, cc = rot(y, dy, 4), rot(c, dc, 2)
            send(
                st.at[ch, yy * 2 + cc, pl.ds(a, 1)], rc.at[ch, zh, here, pl.ds(a, 1)],
                in_s.at[ch, n], in_r.at[ch, n], dev(x, zl, yy, 1 - zh, cc),
            )

    def within(ch, a, n):
        for dy, dc in near[1:]:
            yy, cc = rot(y, dy, 4), rot(c, dc, 2)
            send(
                st.at[ch, yy * 2 + cc, pl.ds(a, 2)], rc.at[ch, zh, here, pl.ds(a, 2)],
                in_s.at[ch, n], in_r.at[ch, n], dev(x, zl, yy, zh, cc),
            )
        pltpu.make_async_copy(
            st.at[ch, here, pl.ds(a, 2)], rc.at[ch, zh, here, pl.ds(a, 2)], in_r.at[ch, n]
        ).start()

    def step_i(ch):
        if ch:
            pack(ch, ((Q, q_ref), (K, k_ref)))
        cross(ch, Q, 0)
        within(ch, Q, 1)

    def step_j(ch):
        if ch == 0:
            loads[2].wait()
            loads[3].wait()
        pack(ch, ((G, g_ref), (V, v_ref)))
        cross(ch, G, 2)
        within(ch, G, 3)

    def step_l(ch):
        loads[4].wait()
        sub = lax.broadcasted_iota(jnp.int32, (8, 16), 0) + 8 * (zl % 2)
        lane = lax.broadcasted_iota(jnp.int32, (8, 16), 1)
        for n in range(CH):
            line = l_ref[pl.ds(rot(x, 1, 4) * CH + n, 1), :]
            column = jnp.sum(jnp.where(sub == lane, line, 0.0), axis=1, keepdims=True)
            lsend[n] = jnp.broadcast_to(column, (8, 128))
        send(lsend, lrecv, l_s, l_r, l_to)

    def step_k(ch):
        cross(ch, K, 4)

    def both(ch, a):
        return jnp.concatenate(
            [rc[ch, :, :, a, rp].reshape(256, 128) for rp in range(2)], axis=1
        )

    def half(ch, side, a):
        return jnp.concatenate(
            [rc[ch, side, :, a, rp].reshape(128, 128) for rp in range(2)], axis=1
        )

    def step_a(ch, n):
        a = (Q, G)[n]
        wait(rc.at[ch, zh, :, pl.ds(a, 2)], in_r.at[ch, 2 * n + 1])
        wait(rc.at[ch, 1 - zh, :, pl.ds(a, 1)], in_r.at[ch, 2 * n])
        part = lax.dot_general(
            both(ch, a), half(ch, zh, a + 1), (((1,), (1,)), ((), ())),
            preferred_element_type=F32,
        )
        tt[ch, n] = part.reshape(32, 8, 128)
        send(
            tt.at[ch, n, pl.ds((1 - c) * 16, 16)], c1.at[ch, n],
            core_s.at[ch, n], core_r.at[ch, n], core_peer,
        )

    def step_b(ch, n):
        wait(c1.at[ch, n], core_r.at[ch, n])
        total = tt[ch, n, pl.ds(c * 16, 16)] + c1[ch, n]
        uu[ch, n] = total.reshape(4, 4, 8, 128)
        for d in (2, 1, 3):
            to = rot(x, d, 4)
            send(
                uu.at[ch, n, to], x1.at[ch, n, d - 1], x_s.at[ch, n], x_r.at[ch, n],
                dev(to, zl, y, zh, c),
            )

    def step_c(ch, n):
        wait(x1.at[ch, n], x_r.at[ch, n])
        ww[ch, n] = (uu[ch, n, x] + x1[ch, n, 0]) + (x1[ch, n, 1] + x1[ch, n, 2])
        for d in range(4):
            to = rot(zl, d, 4)
            send(
                ww.at[ch, n, to], z1.at[ch, n, 3 + d], z_s.at[ch, n], z_r.at[ch, n],
                dev(x, to, y, 1 - zh, c),
            )
        for d in range(1, 4):
            to = rot(zl, d, 4)
            send(
                ww.at[ch, n, to], z1.at[ch, n, d - 1], z_s.at[ch, n], z_r.at[ch, n],
                dev(x, to, y, zh, c),
            )

    def sums(ch, n):
        wait(z1.at[ch, n], z_r.at[ch, n])
        own = (ww[ch, n, zl] + z1[ch, n, 0]) + (z1[ch, n, 1] + z1[ch, n, 2])
        other = (z1[ch, n, 3] + z1[ch, n, 4]) + (z1[ch, n, 5] + z1[ch, n, 6])
        return own, other

    def step_p(ch):
        if ch == 0:
            wait(lrecv, l_r)
        own, other = sums(ch, S)
        pp[ch, 0] = jnp.exp(own - lrecv[ch])
        pp[ch, 1] = jnp.exp(other - lrecv[ch])

    def gather_z(mine, swapped, dst, ssem, rsem):
        for n, step in enumerate((2, 1, 7)):
            to_zl, to_zh = along(step)
            target = dev(x, to_zl, y, to_zh, c)

            @pl.when(to_zh == zh)
            def _():
                send(mine, dst, ssem.at[n], rsem.at[n], target)

            @pl.when(to_zh != zh)
            def _():
                send(swapped, dst, ssem.at[n], rsem.at[n], target)

    def gather_x(whole, got, ssem, rsem, z_recv):
        for n, step in enumerate((6, 7, 1)):
            wait(got(c, x, along(step)[0]), z_recv.at[n])
        block = whole.at[c, x]
        for n, d in enumerate((2, 1, 3)):
            send(block, block, ssem.at[n], rsem.at[n], dev(rot(x, d, 4), zl, y, zh, c))

    def gather_core(whole, ssem, rsem, x_recv):
        for n, d in enumerate((2, 3, 1)):
            wait(whole.at[c, rot(x, d, 4)], x_recv.at[n])
        send(whole.at[c], whole.at[c], ssem, rsem, core_peer)

    def step_dp(ch):
        for side, place in ((0, agp.at[c, x, zl]), (1, psend)):
            place[0] = jnp.concatenate([pp[0, side], pp[1, side]], axis=0).astype(BF16)
            place[1] = jnp.concatenate([pp[2, side], pp[2, side]], axis=0).astype(BF16)
        gather_z(agp.at[c, x, zl], psend, agp.at[c, x, zl], gp_s.at[0], gp_r.at[0])

    def step_ep(ch):
        gather_x(agp, lambda *at: agp.at[at], gp_s.at[1], gp_r.at[1], gp_r.at[0])

    def step_fp(ch):
        gather_core(agp, gp_s.at[2, 0], gp_r.at[2, 0], gp_r.at[1])

    def step_dd(ch):
        own, other = sums(ch, D)
        p_own, p_other = pp[ch, 0], pp[ch, 1]
        delta = jnp.sum(p_own * own + p_other * other, axis=1, keepdims=True)
        d_own = p_own * (own - delta)
        d_other = p_other * (other - delta)
        place = agd.at[ch, c, x, zl]
        place[...] = jnp.concatenate([d_own, d_other], axis=0).astype(BF16)
        dsend[ch] = jnp.concatenate([d_other, d_own], axis=0).astype(BF16)
        gather_z(place, dsend.at[ch], place, gd_s.at[ch, 0], gd_r.at[ch, 0])

    def step_ed(ch):
        gather_x(
            agd.at[ch], lambda *at: agd.at[(ch, *at)], gd_s.at[ch, 1], gd_r.at[ch, 1], gd_r.at[ch, 0]
        )

    def step_fd(ch):
        gather_core(agd.at[ch], gd_s.at[ch, 2, 0], gd_r.at[ch, 2, 0], gd_r.at[ch, 1])

    down = (((0,), (0,)), ((), ()))
    across = (((1,), (0,)), ((), ()))

    def put(ch, a, value):
        for rp in range(2):
            piece = value[:, rp * 128 : rp * 128 + 128].astype(BF16)
            oo[ch, :, a, rp] = piece.reshape(8, 16, 128)

    def give(ch, part, n):
        for dy, dc in near[1:]:
            yy, cc = rot(y, dy, 4), rot(c, dc, 2)
            send(
                oo.at[ch, yy * 2 + cc, part], orr.at[ch, here, part],
                out_s.at[ch, n], out_r.at[ch, n], dev(x, zl, yy, zh, cc),
            )
        pltpu.make_async_copy(
            oo.at[ch, here, part], orr.at[ch, here, part], out_r.at[ch, n]
        ).start()

    def step_gp(ch):
        if ch == 0:
            wait(agp.at[1 - c], gp_r.at[2, 0])
        tile = agp[:, :, :, ch // 2].reshape(32, 16, 128).astype(F32)
        start = 8 * (ch % 2)
        weights = tile[:, start : start + 8].reshape(256, 128).astype(BF16)
        put(ch, 2, lax.dot_general(weights, both(ch, G), down, preferred_element_type=F32))
        give(ch, pl.ds(2, 1), 0)

    def step_gd(ch):
        wait(agd.at[ch, 1 - c], gd_r.at[ch, 2, 0])
        tile = agd[ch].reshape(32, 16, 128).astype(F32)
        slopes = tile[:, :8].reshape(256, 128).astype(BF16)
        put(ch, 1, lax.dot_general(slopes, both(ch, Q), down, preferred_element_type=F32))
        wait(rc.at[ch, 1 - zh, :, pl.ds(K, 1)], in_r.at[ch, 4])
        mine = agd[ch, zh].reshape(16, 16, 128).astype(F32)
        own = mine[:, :8].reshape(128, 128).astype(BF16)
        other = mine[:, 8:].reshape(128, 128).astype(BF16)
        dq = lax.dot_general(own, half(ch, zh, K), across, preferred_element_type=F32)
        dq += lax.dot_general(other, half(ch, 1 - zh, K), across, preferred_element_type=F32)
        put(ch, 0, dq)
        give(ch, pl.ds(0, 2), 1)

    def unpack(a, ref, hbm):
        for tile in range(6):
            pair = []
            for head in (2 * tile, 2 * tile + 1):
                yy, ch = head // CH, head % CH
                pair.append(orr[ch, pl.ds(yy * 2, 2), a].reshape(4, 16, 128))
            first, second = swap_halves(*pair)
            lanes = pl.ds(tile * 128, 128)
            for n in range(4):
                ref[2 * n, :, lanes] = first[n]
                ref[2 * n + 1, :, lanes] = second[n]
        pltpu.make_async_copy(ref, hbm, store_s.at[a]).start()

    def step_hp(ch):
        for n in range(CH):
            wait(orr.at[n, :, pl.ds(2, 1)], out_r.at[n, 0])
        unpack(2, dv_ref, dv_hbm)

    def step_hd(ch):
        for n in range(CH):
            wait(orr.at[n, :, pl.ds(0, 2)], out_r.at[n, 1])
        unpack(1, dk_ref, dk_hbm)
        unpack(0, dq_ref, dq_hbm)

    steps = {
        "I": step_i, "J": step_j, "K": step_k, "L": step_l,
        "As": lambda ch: step_a(ch, S), "Ad": lambda ch: step_a(ch, D),
        "Bs": lambda ch: step_b(ch, S), "Bd": lambda ch: step_b(ch, D),
        "Cs": lambda ch: step_c(ch, S), "Cd": lambda ch: step_c(ch, D),
        "Ds": step_p, "Dp": step_dp, "Ep": step_ep, "Fp": step_fp, "Gp": step_gp, "Hp": step_hp,
        "Dd": step_dd, "Ed": step_ed, "Fd": step_fd, "Gd": step_gd, "Hd": step_hd,
    }
    for name in ORDER:
        steps[name[:-1]](int(name[-1]))

    wait(lsend, l_s)
    wait(agp.at[c], gp_s.at[2, 0])
    for n in range(3):
        wait(agp.at[c, x, zl], gp_s.at[0, n])
        wait(agp.at[c, x], gp_s.at[1, n])
    for ch in range(CH):
        for a, n in ((Q, 0), (G, 2), (K, 4)):
            wait(st.at[ch, :, pl.ds(a, 1)], in_s.at[ch, n])
        for a, n in ((Q, 1), (G, 3)):
            wait(st.at[ch, pl.ds(0, 7), pl.ds(a, 2)], in_s.at[ch, n])
        for n in range(2):
            wait(c1.at[ch, n], core_s.at[ch, n])
            wait(x1.at[ch, n], x_s.at[ch, n])
            wait(z1.at[ch, n], z_s.at[ch, n])
        for n in range(3):
            wait(agd.at[ch, c, x, zl], gd_s.at[ch, 0, n])
            wait(agd.at[ch, c, x], gd_s.at[ch, 1, n])
        wait(agd.at[ch, c], gd_s.at[ch, 2, 0])
        wait(oo.at[ch, pl.ds(0, 7), pl.ds(2, 1)], out_s.at[ch, 0])
        wait(oo.at[ch, pl.ds(0, 7), pl.ds(0, 2)], out_s.at[ch, 1])
    for a, (ref, hbm) in enumerate(((dq_ref, dq_hbm), (dk_ref, dk_hbm), (dv_ref, dv_hbm))):
        pltpu.make_async_copy(ref, hbm, store_s.at[a]).wait()


def body(query_proj, key_proj, value_proj, grad_output, log_totals):
    dma = pltpu.SemaphoreType.DMA
    anywhere = pl.BlockSpec(memory_space=pl.ANY)
    return pl.pallas_call(
        kernel,
        out_shape=[jax.ShapeDtypeStruct(query_proj.shape, BF16)] * 3,
        in_specs=[anywhere] * 5,
        out_specs=[anywhere] * 3,
        scratch_shapes=[
            *[pltpu.VMEM(query_proj.shape, BF16)] * 4,
            pltpu.VMEM(log_totals.shape, F32),
            *[pltpu.VMEM(query_proj.shape, BF16)] * 3,
            dma((5,)), dma((3,)),
            pltpu.VMEM((CH, 8, 4, 2, 16, 128), BF16),
            pltpu.VMEM((CH, 2, 8, 4, 2, 16, 128), BF16),
            pltpu.VMEM((CH, 2, 32, 8, 128), F32),
            pltpu.VMEM((CH, 2, 16, 8, 128), F32),
            pltpu.VMEM((CH, 2, 4, 4, 8, 128), F32),
            pltpu.VMEM((CH, 2, 3, 4, 8, 128), F32),
            pltpu.VMEM((CH, 2, 4, 8, 128), F32),
            pltpu.VMEM((CH, 2, 7, 8, 128), F32),
            pltpu.VMEM((CH, 2, 8, 128), F32),
            pltpu.VMEM((2, 4, 4, 2, 16, 128), BF16),
            pltpu.VMEM((2, 16, 128), BF16),
            pltpu.VMEM((CH, 2, 4, 4, 16, 128), BF16),
            pltpu.VMEM((CH, 16, 128), BF16),
            pltpu.VMEM((CH, 8, 3, 2, 16, 128), BF16),
            pltpu.VMEM((CH, 8, 3, 2, 16, 128), BF16),
            pltpu.VMEM((CH, 8, 128), F32),
            pltpu.VMEM((CH, 8, 128), F32),
            dma((CH, 5)), dma((CH, 5)),
            dma((CH, 2)), dma((CH, 2)),
            dma((CH, 2)), dma((CH, 2)),
            dma((CH, 2)), dma((CH, 2)),
            dma((3, 3)), dma((3, 3)),
            dma((CH, 3, 3)), dma((CH, 3, 3)),
            dma((CH, 2)), dma((CH, 2)),
            dma, dma,
        ],
        compiler_params=pltpu.CompilerParams(
            collective_id=0, has_side_effects=True, vmem_limit_bytes=60 * 2**20
        ),
        name="tied_row_backward",
    )(query_proj, key_proj, value_proj, grad_output, log_totals)


def solution(mesh):
    in_specs = (
        P("row", "col", None),
        P("row", "col", None),
        P("row", "col", None),
        P("row", "col", None),
        P(None, "col"),
    )
    out_specs = (P("row", "col", None), P("row", "col", None), P("row", "col", None))
    return jax.shard_map(body, mesh=mesh, in_specs=in_specs, out_specs=out_specs, check_vma=False)
```

```python
import jax
import jax.numpy as jnp
from jax import lax
from jax.experimental import pallas as pl
from jax.experimental.pallas import tpu as pltpu
from jax.sharding import PartitionSpec as P

MESH = pl.DeviceIdType.MESH
NY, NC = 4, 2
CH = 3
F32, BF16 = jnp.float32, jnp.bfloat16
Q, K, G, V = 0, 1, 2, 3
S, D = 0, 1

ORDER = (
    "I0", "L0", "I1", "I2", "J0", "J1", "J2", "As0", "Bs0", "As1", "Bs1", "As2", "Bs2", "Cs0",
    "Cs1", "Cs2", "K0", "K1", "Ad0", "Ad1", "Cd0", "Ad2", "Cd1", "Cd2", "Ds0", "Ds1", "Ds2", "Dp0",
    "Dd0", "Dd1", "Dd2", "K2", "Ep0", "Ed0", "Ed1", "Ed2", "Fp0", "Fd0", "Fd1", "Fd2", "Gp0", "Gp1",
    "Gp2", "Gd0", "Gd1", "Gd2", "Hp0", "Hd0",
)


def swap_halves(low, high):
    first = jnp.concatenate([low[..., :64], high[..., :64]], axis=-1)
    second = jnp.concatenate([low[..., 64:], high[..., 64:]], axis=-1)
    return first, second


def kernel(
    q_hbm, k_hbm, v_hbm, g_hbm, l_hbm, orr,
    q_ref, k_ref, v_ref, g_ref, l_ref, load_s,
    st, rc, tt, tb, xb, c1, uu, x1, ww, z1, pp, agp, psend, agd, dsend, oo, lsend, lrecv,
    in_s, in_r, core_s, core_r, x_s, x_r, z_s, z_r, gp_s, gp_r, gd_s, gd_r, out_s, out_r, l_s, l_r,
):
    row, col = lax.axis_index("row"), lax.axis_index("col")
    x, zl = row // 4, row % 4
    y, zh, c = col // 4, (col // 2) % 2, col % 2
    here = y * 2 + c

    def dev(x, zl, y, zh, c):
        return (x * 4 + zl, (y * 2 + zh) * 2 + c)

    def send(src, dst, ssem, rsem, target):
        pltpu.make_async_remote_copy(
            src, dst, ssem, rsem, device_id=target, device_id_type=MESH
        ).start()

    def wait(ref, sem):
        pltpu.make_async_copy(ref, ref, sem).wait()

    def rot(value, step, count):
        return lax.rem(value + step, count)

    loads = [
        pltpu.make_async_copy(src, dst, load_s.at[n])
        for n, (src, dst) in enumerate((
            (q_hbm, q_ref), (k_hbm, k_ref), (g_hbm, g_ref), (v_hbm, v_ref), (l_hbm, l_ref)
        ))
    ]
    for load in loads:
        load.start()

    others = [(dx, dc) for dx in (2, 1, 3, 0) for dc in (1, 0) if dx or dc]
    near = [(dy, dc) for dy in range(NY) for dc in range(NC)]
    core_peer = dev(x, zl, y, zh, 1 - c)

    def along(step):
        z = rot(zh * 4 + zl, step, 8)
        return z % 4, z // 4

    l_to = dev(y, 2 * c + zl % 2, rot(x, 1, 4), zl // 2, zh)
    l_from = dev(rot(y, 3, 4), zh * 2 + zl % 2, x, c, zl // 2)

    barrier = pltpu.get_barrier_semaphore()
    peers = [dev(x, zl, rot(y, dy, 4), zh, rot(c, dc, 2)) for dy, dc in near[1:]]
    peers += [dev(x, zl, rot(y, dy, 4), 1 - zh, rot(c, dc, 2)) for dy, dc in near]
    peers += [dev(rot(x, d, 4), zl, y, zh, c) for d in range(1, 4)]
    peers += [dev(rot(x, d, 4), zl, y, zh, 1 - c) for d in range(1, 4)]
    peers += [dev(x, rot(zl, d, 4), y, zh, c) for d in range(1, 4)]
    peers += [dev(x, rot(zl, d, 4), y, 1 - zh, c) for d in range(1, 4)]
    peers += [l_from]
    for peer in peers:
        pl.semaphore_signal(barrier, inc=1, device_id=peer, device_id_type=MESH)

    def pack(ch, arrays):
        for a, ref in arrays:
            for yy in range(NY):
                head = yy * CH + ch
                tile = head // 2
                part = ref[:, :, tile * 128 : tile * 128 + 128].reshape(4, 2, 16, 128)
                block = swap_halves(part[:, 0], part[:, 1])[head % 2]
                for cc in range(NC):
                    st[ch, yy * 2 + cc, a] = block[2 * cc : 2 * cc + 2]

    loads[0].wait()
    loads[1].wait()
    pack(0, ((Q, q_ref), (K, k_ref)))
    pl.semaphore_wait(barrier, len(peers))

    def cross(ch, a, n):
        for dy, dc in near:
            yy, cc = rot(y, dy, 4), rot(c, dc, 2)
            send(
                st.at[ch, yy * 2 + cc, pl.ds(a, 1)], rc.at[ch, zh, here, pl.ds(a, 1)],
                in_s.at[ch, n], in_r.at[ch, n], dev(x, zl, yy, 1 - zh, cc),
            )

    def within(ch, a, n):
        for dy, dc in near[1:]:
            yy, cc = rot(y, dy, 4), rot(c, dc, 2)
            send(
                st.at[ch, yy * 2 + cc, pl.ds(a, 2)], rc.at[ch, zh, here, pl.ds(a, 2)],
                in_s.at[ch, n], in_r.at[ch, n], dev(x, zl, yy, zh, cc),
            )
        pltpu.make_async_copy(
            st.at[ch, here, pl.ds(a, 2)], rc.at[ch, zh, here, pl.ds(a, 2)], in_r.at[ch, n]
        ).start()

    def step_i(ch):
        if ch:
            pack(ch, ((Q, q_ref), (K, k_ref)))
        cross(ch, Q, 0)
        within(ch, Q, 1)

    def step_j(ch):
        if ch == 0:
            loads[2].wait()
            loads[3].wait()
        pack(ch, ((G, g_ref), (V, v_ref)))
        cross(ch, G, 2)
        within(ch, G, 3)

    def step_l(ch):
        loads[4].wait()
        sub = lax.broadcasted_iota(jnp.int32, (8, 16), 0) + 8 * (zl % 2)
        lane = lax.broadcasted_iota(jnp.int32, (8, 16), 1)
        for n in range(CH):
            line = l_ref[pl.ds(rot(x, 1, 4) * CH + n, 1), :]
            column = jnp.sum(jnp.where(sub == lane, line, 0.0), axis=1, keepdims=True)
            lsend[n] = jnp.broadcast_to(column, (8, 128))
        send(lsend, lrecv, l_s, l_r, l_to)

    def step_k(ch):
        cross(ch, K, 4)

    def both(ch, a):
        return jnp.concatenate(
            [rc[ch, :, :, a, rp].reshape(256, 128) for rp in range(2)], axis=1
        )

    def half(ch, side, a):
        return jnp.concatenate(
            [rc[ch, side, :, a, rp].reshape(128, 128) for rp in range(2)], axis=1
        )

    def step_a(ch, n):
        a = (Q, G)[n]
        wait(rc.at[ch, zh, :, pl.ds(a, 2)], in_r.at[ch, 2 * n + 1])
        wait(rc.at[ch, 1 - zh, :, pl.ds(a, 1)], in_r.at[ch, 2 * n])
        part = lax.dot_general(
            both(ch, a), half(ch, zh, a + 1), (((1,), (1,)), ((), ())),
            preferred_element_type=F32,
        )
        tt[ch, n] = part.reshape(32, 8, 128)
        if n == D:
            tb[ch] = part.astype(BF16).reshape(8, 32, 128)
            for k, (dx, dc) in enumerate(others):
                to_x, to_c = rot(x, dx, 4), rot(c, dc, 2)
                send(
                    tb.at[ch, to_c * 4 + to_x], xb.at[ch, k], x_s.at[ch, n], x_r.at[ch, n],
                    dev(to_x, zl, y, zh, to_c),
                )
            return
        send(
            tt.at[ch, n, pl.ds((1 - c) * 16, 16)], c1.at[ch], core_s.at[ch], core_r.at[ch], core_peer,
        )

    def step_b(ch, n):
        wait(c1.at[ch], core_r.at[ch])
        total = tt[ch, n, pl.ds(c * 16, 16)] + c1[ch]
        uu[ch] = total.reshape(4, 4, 8, 128)
        for d in (2, 1, 3):
            to = rot(x, d, 4)
            send(
                uu.at[ch, to], x1.at[ch, d - 1], x_s.at[ch, n], x_r.at[ch, n],
                dev(to, zl, y, zh, c),
            )

    def step_c(ch, n):
        if n == D:
            wait(xb.at[ch], x_r.at[ch, n])
            part = [xb[ch, k].astype(F32) for k in range(7)]
            total = ((part[0] + part[1]) + (part[2] + part[3])) + ((part[4] + part[5]) + part[6])
            ww[ch, n] = tt[ch, n, pl.ds(c * 16 + x * 4, 4)] + total.reshape(4, 8, 128)
        else:
            wait(x1.at[ch], x_r.at[ch, n])
            ww[ch, n] = (uu[ch, x] + x1[ch, 0]) + (x1[ch, 1] + x1[ch, 2])
        for d in range(4):
            to = rot(zl, d, 4)
            send(
                ww.at[ch, n, to], z1.at[ch, n, 3 + d], z_s.at[ch, n], z_r.at[ch, n],
                dev(x, to, y, 1 - zh, c),
            )
        for d in range(1, 4):
            to = rot(zl, d, 4)
            send(
                ww.at[ch, n, to], z1.at[ch, n, d - 1], z_s.at[ch, n], z_r.at[ch, n],
                dev(x, to, y, zh, c),
            )

    def sums(ch, n):
        wait(z1.at[ch, n], z_r.at[ch, n])
        own = (ww[ch, n, zl] + z1[ch, n, 0]) + (z1[ch, n, 1] + z1[ch, n, 2])
        other = (z1[ch, n, 3] + z1[ch, n, 4]) + (z1[ch, n, 5] + z1[ch, n, 6])
        return own, other

    def step_p(ch):
        if ch == 0:
            wait(lrecv, l_r)
        own, other = sums(ch, S)
        pp[ch, 0] = jnp.exp(own - lrecv[ch])
        pp[ch, 1] = jnp.exp(other - lrecv[ch])

    def gather_z(mine, swapped, dst, ssem, rsem):
        for n, step in enumerate((2, 1, 7)):
            to_zl, to_zh = along(step)
            target = dev(x, to_zl, y, to_zh, c)

            @pl.when(to_zh == zh)
            def _():
                send(mine, dst, ssem.at[n], rsem.at[n], target)

            @pl.when(to_zh != zh)
            def _():
                send(swapped, dst, ssem.at[n], rsem.at[n], target)

    def gather_x(whole, got, ssem, rsem, z_recv):
        for n, step in enumerate((6, 7, 1)):
            wait(got(c, x, along(step)[0]), z_recv.at[n])
        block = whole.at[c, x]
        for n, d in enumerate((2, 1, 3)):
            send(block, block, ssem.at[n], rsem.at[n], dev(rot(x, d, 4), zl, y, zh, c))

    def gather_core(whole, ssem, rsem, x_recv):
        for n, d in enumerate((2, 3, 1)):
            wait(whole.at[c, rot(x, d, 4)], x_recv.at[n])
        send(whole.at[c], whole.at[c], ssem, rsem, core_peer)

    def step_dp(ch):
        for side, place in ((0, agp.at[c, x, zl]), (1, psend)):
            place[0] = jnp.concatenate([pp[0, side], pp[1, side]], axis=0).astype(BF16)
            place[1] = jnp.concatenate([pp[2, side], pp[2, side]], axis=0).astype(BF16)
        gather_z(agp.at[c, x, zl], psend, agp.at[c, x, zl], gp_s.at[0], gp_r.at[0])

    def step_ep(ch):
        gather_x(agp, lambda *at: agp.at[at], gp_s.at[1], gp_r.at[1], gp_r.at[0])

    def step_fp(ch):
        gather_core(agp, gp_s.at[2, 0], gp_r.at[2, 0], gp_r.at[1])

    def step_dd(ch):
        own, other = sums(ch, D)
        p_own, p_other = pp[ch, 0], pp[ch, 1]
        delta = jnp.sum(p_own * own + p_other * other, axis=1, keepdims=True)
        d_own = p_own * (own - delta)
        d_other = p_other * (other - delta)
        place = agd.at[ch, c, x, zl]
        place[...] = jnp.concatenate([d_own, d_other], axis=0).astype(BF16)
        dsend[ch] = jnp.concatenate([d_other, d_own], axis=0).astype(BF16)
        gather_z(place, dsend.at[ch], place, gd_s.at[ch, 0], gd_r.at[ch, 0])

    def step_ed(ch):
        gather_x(
            agd.at[ch], lambda *at: agd.at[(ch, *at)], gd_s.at[ch, 1], gd_r.at[ch, 1], gd_r.at[ch, 0]
        )

    def step_fd(ch):
        gather_core(agd.at[ch], gd_s.at[ch, 2, 0], gd_r.at[ch, 2, 0], gd_r.at[ch, 1])

    down = (((0,), (0,)), ((), ()))
    across = (((1,), (0,)), ((), ()))

    def put(ch, a, value):
        for rp in range(2):
            piece = value[:, rp * 128 : rp * 128 + 128].astype(BF16)
            oo[ch, :, a, rp] = piece.reshape(8, 16, 128)

    def give(ch, part, n):
        for dy, dc in near[1:]:
            yy, cc = rot(y, dy, 4), rot(c, dc, 2)
            send(
                oo.at[ch, yy * 2 + cc, part], orr.at[ch, here, part],
                out_s.at[ch, n], out_r.at[ch, n], dev(x, zl, yy, zh, cc),
            )
        pltpu.make_async_copy(
            oo.at[ch, here, part], orr.at[ch, here, part], out_r.at[ch, n]
        ).start()

    def step_gp(ch):
        if ch == 0:
            wait(agp.at[1 - c], gp_r.at[2, 0])
        tile = agp[:, :, :, ch // 2].reshape(32, 16, 128).astype(F32)
        start = 8 * (ch % 2)
        weights = tile[:, start : start + 8].reshape(256, 128).astype(BF16)
        put(ch, 2, lax.dot_general(weights, both(ch, G), down, preferred_element_type=F32))
        give(ch, pl.ds(2, 1), 0)

    def step_gd(ch):
        wait(agd.at[ch, 1 - c], gd_r.at[ch, 2, 0])
        tile = agd[ch].reshape(32, 16, 128).astype(F32)
        slopes = tile[:, :8].reshape(256, 128).astype(BF16)
        put(ch, 1, lax.dot_general(slopes, both(ch, Q), down, preferred_element_type=F32))
        wait(rc.at[ch, 1 - zh, :, pl.ds(K, 1)], in_r.at[ch, 4])
        mine = agd[ch, zh].reshape(16, 16, 128).astype(F32)
        own = mine[:, :8].reshape(128, 128).astype(BF16)
        other = mine[:, 8:].reshape(128, 128).astype(BF16)
        dq = lax.dot_general(own, half(ch, zh, K), across, preferred_element_type=F32)
        dq += lax.dot_general(other, half(ch, 1 - zh, K), across, preferred_element_type=F32)
        put(ch, 0, dq)
        give(ch, pl.ds(0, 2), 1)

    def step_hp(ch):
        for n in range(CH):
            wait(orr.at[n, :, pl.ds(2, 1)], out_r.at[n, 0])

    def step_hd(ch):
        for n in range(CH):
            wait(orr.at[n, :, pl.ds(0, 2)], out_r.at[n, 1])

    steps = {
        "I": step_i, "J": step_j, "K": step_k, "L": step_l,
        "As": lambda ch: step_a(ch, S), "Ad": lambda ch: step_a(ch, D),
        "Bs": lambda ch: step_b(ch, S),
        "Cs": lambda ch: step_c(ch, S), "Cd": lambda ch: step_c(ch, D),
        "Ds": step_p, "Dp": step_dp, "Ep": step_ep, "Fp": step_fp, "Gp": step_gp, "Hp": step_hp,
        "Dd": step_dd, "Ed": step_ed, "Fd": step_fd, "Gd": step_gd, "Hd": step_hd,
    }
    for name in ORDER:
        steps[name[:-1]](int(name[-1]))

    wait(lsend, l_s)
    wait(agp.at[c], gp_s.at[2, 0])
    for n in range(3):
        wait(agp.at[c, x, zl], gp_s.at[0, n])
        wait(agp.at[c, x], gp_s.at[1, n])
    for ch in range(CH):
        for a, n in ((Q, 0), (G, 2), (K, 4)):
            wait(st.at[ch, :, pl.ds(a, 1)], in_s.at[ch, n])
        for a, n in ((Q, 1), (G, 3)):
            wait(st.at[ch, pl.ds(0, 7), pl.ds(a, 2)], in_s.at[ch, n])
        wait(c1.at[ch], core_s.at[ch])
        wait(x1.at[ch], x_s.at[ch, S])
        wait(xb.at[ch], x_s.at[ch, D])
        for n in range(2):
            wait(z1.at[ch, n], z_s.at[ch, n])
        for n in range(3):
            wait(agd.at[ch, c, x, zl], gd_s.at[ch, 0, n])
            wait(agd.at[ch, c, x], gd_s.at[ch, 1, n])
        wait(agd.at[ch, c], gd_s.at[ch, 2, 0])
        wait(oo.at[ch, pl.ds(0, 7), pl.ds(2, 1)], out_s.at[ch, 0])
        wait(oo.at[ch, pl.ds(0, 7), pl.ds(0, 2)], out_s.at[ch, 1])


def unpack(packed, dq_hbm, dk_hbm, dv_hbm, got, done, load_s, store_s):
    out = (dq_hbm, dk_hbm, dv_hbm)
    loads = [pltpu.make_async_copy(packed.at[:, :, a], got.at[a], load_s.at[a]) for a in range(3)]
    stores = [pltpu.make_async_copy(done.at[a], out[a], store_s.at[a]) for a in range(3)]
    for load in loads:
        load.start()
    for a in range(3):
        loads[a].wait()
        for tile in range(6):
            pair = []
            for head in (2 * tile, 2 * tile + 1):
                yy, ch = head // CH, head % CH
                pair.append(got[a, ch, pl.ds(yy * 2, 2)].reshape(4, 16, 128))
            first, second = swap_halves(*pair)
            lanes = pl.ds(tile * 128, 128)
            for n in range(4):
                done[a, 2 * n, :, lanes] = first[n]
                done[a, 2 * n + 1, :, lanes] = second[n]
        stores[a].start()
    for store in stores:
        store.wait()


def body(query_proj, key_proj, value_proj, grad_output, log_totals):
    dma = pltpu.SemaphoreType.DMA
    anywhere = pl.BlockSpec(memory_space=pl.ANY)
    packed = pl.pallas_call(
        kernel,
        out_shape=jax.ShapeDtypeStruct((CH, 8, 3, 2, 16, 128), BF16),
        in_specs=[anywhere] * 5,
        out_specs=anywhere,
        scratch_shapes=[
            *[pltpu.VMEM(query_proj.shape, BF16)] * 4,
            pltpu.VMEM(log_totals.shape, F32),
            dma((5,)),
            pltpu.VMEM((CH, 8, 4, 2, 16, 128), BF16),
            pltpu.VMEM((CH, 2, 8, 4, 2, 16, 128), BF16),
            pltpu.VMEM((CH, 2, 32, 8, 128), F32),
            pltpu.VMEM((CH, 8, 32, 128), BF16),
            pltpu.VMEM((CH, 7, 32, 128), BF16),
            pltpu.VMEM((CH, 16, 8, 128), F32),
            pltpu.VMEM((CH, 4, 4, 8, 128), F32),
            pltpu.VMEM((CH, 3, 4, 8, 128), F32),
            pltpu.VMEM((CH, 2, 4, 8, 128), F32),
            pltpu.VMEM((CH, 2, 7, 8, 128), F32),
            pltpu.VMEM((CH, 2, 8, 128), F32),
            pltpu.VMEM((2, 4, 4, 2, 16, 128), BF16),
            pltpu.VMEM((2, 16, 128), BF16),
            pltpu.VMEM((CH, 2, 4, 4, 16, 128), BF16),
            pltpu.VMEM((CH, 16, 128), BF16),
            pltpu.VMEM((CH, 8, 3, 2, 16, 128), BF16),
            pltpu.VMEM((CH, 8, 128), F32),
            pltpu.VMEM((CH, 8, 128), F32),
            dma((CH, 5)), dma((CH, 5)),
            dma((CH,)), dma((CH,)),
            dma((CH, 2)), dma((CH, 2)),
            dma((CH, 2)), dma((CH, 2)),
            dma((3, 3)), dma((3, 3)),
            dma((CH, 3, 3)), dma((CH, 3, 3)),
            dma((CH, 2)), dma((CH, 2)),
            dma, dma,
        ],
        compiler_params=pltpu.CompilerParams(
            collective_id=0, has_side_effects=True, vmem_limit_bytes=60 * 2**20
        ),
        name="tied_row_backward",
    )(query_proj, key_proj, value_proj, grad_output, log_totals)
    return pl.pallas_call(
        unpack,
        out_shape=[jax.ShapeDtypeStruct(query_proj.shape, BF16)] * 3,
        in_specs=[anywhere],
        out_specs=[anywhere] * 3,
        scratch_shapes=[
            pltpu.VMEM((3, CH, 8, 2, 16, 128), BF16),
            pltpu.VMEM((3, *query_proj.shape), BF16),
            dma((3,)), dma((3,)),
        ],
        compiler_params=pltpu.CompilerParams(vmem_limit_bytes=60 * 2**20),
        name="unpack_gradients",
    )(packed)


def solution(mesh):
    in_specs = (
        P("row", "col", None),
        P("row", "col", None),
        P("row", "col", None),
        P("row", "col", None),
        P(None, "col"),
    )
    out_specs = (P("row", "col", None), P("row", "col", None), P("row", "col", None))
    return jax.shard_map(body, mesh=mesh, in_specs=in_specs, out_specs=out_specs, check_vma=False)
```

```python
import jax
import jax.numpy as jnp
from jax import lax
from jax.experimental import pallas as pl
from jax.experimental.pallas import tpu as pltpu
from jax.sharding import PartitionSpec as P

MESH = pl.DeviceIdType.MESH
NY, NC = 4, 2
CH = 3
F32, BF16 = jnp.float32, jnp.bfloat16
Q, K, G, V = 0, 1, 2, 3
S, D = 0, 1

ORDER = (
    "I0", "L0", "I1", "I2", "J0", "J1", "J2", "As0", "Bs0", "As1", "Bs1", "As2", "Bs2", "Cs0",
    "Cs1", "Cs2", "K0", "K1", "Ad0", "Ad1", "Cd0", "Ad2", "Cd1", "Cd2", "K2", "Ds0", "Ds1", "Ds2",
    "Dp0", "Dd0", "Dd1", "Dd2", "Ep0", "Ed0", "Ed1", "Ed2", "Fp0", "Fd0", "Fd1", "Fd2", "Gp0", "Gp1",
    "Gp2", "Gd0", "Gd1", "Gd2", "Hp0", "Hd0",
)


def swap_halves(low, high):
    first = jnp.concatenate([low[..., :64], high[..., :64]], axis=-1)
    second = jnp.concatenate([low[..., 64:], high[..., 64:]], axis=-1)
    return first, second


def kernel(
    q_hbm, k_hbm, v_hbm, g_hbm, l_hbm, orr,
    q_ref, k_ref, v_ref, g_ref, l_ref, load_s,
    st, rc, tt, tb, xb, c1, uu, x1, ww, z1, pp, agp, psend, agd, dsend, oo, lsend, lrecv,
    in_s, in_r, core_s, core_r, x_s, x_r, z_s, z_r, gp_s, gp_r, gd_s, gd_r, out_s, out_r, l_s, l_r,
):
    row, col = lax.axis_index("row"), lax.axis_index("col")
    x, zl = row // 4, row % 4
    y, zh, c = col // 4, (col // 2) % 2, col % 2
    here = y * 2 + c

    def dev(x, zl, y, zh, c):
        return (x * 4 + zl, (y * 2 + zh) * 2 + c)

    def send(src, dst, ssem, rsem, target):
        pltpu.make_async_remote_copy(
            src, dst, ssem, rsem, device_id=target, device_id_type=MESH
        ).start()

    def wait(ref, sem):
        pltpu.make_async_copy(ref, ref, sem).wait()

    def rot(value, step, count):
        return lax.rem(value + step, count)

    loads = [
        pltpu.make_async_copy(src, dst, load_s.at[n])
        for n, (src, dst) in enumerate((
            (q_hbm, q_ref), (k_hbm, k_ref), (g_hbm, g_ref), (v_hbm, v_ref), (l_hbm, l_ref)
        ))
    ]
    for load in loads:
        load.start()

    others = [(dx, dc) for dx in (2, 1, 3, 0) for dc in (1, 0) if dx or dc]
    near = [(dy, dc) for dy in range(NY) for dc in range(NC)]
    core_peer = dev(x, zl, y, zh, 1 - c)

    def along(step):
        z = rot(zh * 4 + zl, step, 8)
        return z % 4, z // 4

    l_to = dev(y, 2 * c + zl % 2, rot(x, 1, 4), zl // 2, zh)
    l_from = dev(rot(y, 3, 4), zh * 2 + zl % 2, x, c, zl // 2)

    barrier = pltpu.get_barrier_semaphore()
    peers = [dev(x, zl, rot(y, dy, 4), zh, rot(c, dc, 2)) for dy, dc in near[1:]]
    peers += [dev(x, zl, rot(y, dy, 4), 1 - zh, rot(c, dc, 2)) for dy, dc in near]
    peers += [dev(rot(x, d, 4), zl, y, zh, c) for d in range(1, 4)]
    peers += [dev(rot(x, d, 4), zl, y, zh, 1 - c) for d in range(1, 4)]
    peers += [dev(x, rot(zl, d, 4), y, zh, c) for d in range(1, 4)]
    peers += [dev(x, rot(zl, d, 4), y, 1 - zh, c) for d in range(1, 4)]
    peers += [l_from]
    for peer in peers:
        pl.semaphore_signal(barrier, inc=1, device_id=peer, device_id_type=MESH)

    def pack(ch, arrays):
        for a, ref in arrays:
            for yy in range(NY):
                head = yy * CH + ch
                tile = head // 2
                part = ref[:, :, tile * 128 : tile * 128 + 128].reshape(4, 2, 16, 128)
                block = swap_halves(part[:, 0], part[:, 1])[head % 2]
                for cc in range(NC):
                    st[ch, yy * 2 + cc, a] = block[2 * cc : 2 * cc + 2]

    loads[0].wait()
    loads[1].wait()
    pack(0, ((Q, q_ref), (K, k_ref)))
    pl.semaphore_wait(barrier, len(peers))

    def cross(ch, a, n):
        for dy, dc in near:
            yy, cc = rot(y, dy, 4), rot(c, dc, 2)
            send(
                st.at[ch, yy * 2 + cc, pl.ds(a, 1)], rc.at[ch, zh, here, pl.ds(a, 1)],
                in_s.at[ch, n], in_r.at[ch, n], dev(x, zl, yy, 1 - zh, cc),
            )

    def within(ch, a, n):
        for dy, dc in near[1:]:
            yy, cc = rot(y, dy, 4), rot(c, dc, 2)
            send(
                st.at[ch, yy * 2 + cc, pl.ds(a, 2)], rc.at[ch, zh, here, pl.ds(a, 2)],
                in_s.at[ch, n], in_r.at[ch, n], dev(x, zl, yy, zh, cc),
            )
        pltpu.make_async_copy(
            st.at[ch, here, pl.ds(a, 2)], rc.at[ch, zh, here, pl.ds(a, 2)], in_r.at[ch, n]
        ).start()

    def step_i(ch):
        if ch:
            pack(ch, ((Q, q_ref), (K, k_ref)))
        cross(ch, Q, 0)
        within(ch, Q, 1)

    def step_j(ch):
        if ch == 0:
            loads[2].wait()
            loads[3].wait()
        pack(ch, ((G, g_ref), (V, v_ref)))
        cross(ch, G, 2)
        within(ch, G, 3)

    def step_l(ch):
        loads[4].wait()
        sub = lax.broadcasted_iota(jnp.int32, (8, 16), 0) + 8 * (zl % 2)
        lane = lax.broadcasted_iota(jnp.int32, (8, 16), 1)
        for n in range(CH):
            line = l_ref[pl.ds(rot(x, 1, 4) * CH + n, 1), :]
            column = jnp.sum(jnp.where(sub == lane, line, 0.0), axis=1, keepdims=True)
            lsend[n] = jnp.broadcast_to(column, (8, 128))
        send(lsend, lrecv, l_s, l_r, l_to)

    def step_k(ch):
        cross(ch, K, 4)

    def both(ch, a):
        return jnp.concatenate(
            [rc[ch, :, :, a, rp].reshape(256, 128) for rp in range(2)], axis=1
        )

    def half(ch, side, a):
        return jnp.concatenate(
            [rc[ch, side, :, a, rp].reshape(128, 128) for rp in range(2)], axis=1
        )

    def step_a(ch, n):
        a = (Q, G)[n]
        wait(rc.at[ch, zh, :, pl.ds(a, 2)], in_r.at[ch, 2 * n + 1])
        wait(rc.at[ch, 1 - zh, :, pl.ds(a, 1)], in_r.at[ch, 2 * n])
        part = lax.dot_general(
            both(ch, a), half(ch, zh, a + 1), (((1,), (1,)), ((), ())),
            preferred_element_type=F32,
        )
        tt[ch, n] = part.reshape(32, 8, 128)
        if n == D:
            tb[ch] = part.astype(BF16).reshape(8, 32, 128)
            for k, (dx, dc) in enumerate(others):
                to_x, to_c = rot(x, dx, 4), rot(c, dc, 2)
                send(
                    tb.at[ch, to_c * 4 + to_x], xb.at[ch, k], x_s.at[ch, n], x_r.at[ch, n],
                    dev(to_x, zl, y, zh, to_c),
                )
            return
        send(
            tt.at[ch, n, pl.ds((1 - c) * 16, 16)], c1.at[ch], core_s.at[ch], core_r.at[ch], core_peer,
        )

    def step_b(ch, n):
        wait(c1.at[ch], core_r.at[ch])
        total = tt[ch, n, pl.ds(c * 16, 16)] + c1[ch]
        uu[ch] = total.reshape(4, 4, 8, 128)
        for d in (2, 1, 3):
            to = rot(x, d, 4)
            send(
                uu.at[ch, to], x1.at[ch, d - 1], x_s.at[ch, n], x_r.at[ch, n],
                dev(to, zl, y, zh, c),
            )

    def step_c(ch, n):
        if n == D:
            wait(xb.at[ch], x_r.at[ch, n])
            part = [xb[ch, k].astype(F32) for k in range(7)]
            total = ((part[0] + part[1]) + (part[2] + part[3])) + ((part[4] + part[5]) + part[6])
            ww[ch, n] = tt[ch, n, pl.ds(c * 16 + x * 4, 4)] + total.reshape(4, 8, 128)
        else:
            wait(x1.at[ch], x_r.at[ch, n])
            ww[ch, n] = (uu[ch, x] + x1[ch, 0]) + (x1[ch, 1] + x1[ch, 2])
        for d in range(4):
            to = rot(zl, d, 4)
            send(
                ww.at[ch, n, to], z1.at[ch, n, 3 + d], z_s.at[ch, n], z_r.at[ch, n],
                dev(x, to, y, 1 - zh, c),
            )
        for d in range(1, 4):
            to = rot(zl, d, 4)
            send(
                ww.at[ch, n, to], z1.at[ch, n, d - 1], z_s.at[ch, n], z_r.at[ch, n],
                dev(x, to, y, zh, c),
            )

    def sums(ch, n):
        wait(z1.at[ch, n], z_r.at[ch, n])
        own = (ww[ch, n, zl] + z1[ch, n, 0]) + (z1[ch, n, 1] + z1[ch, n, 2])
        other = (z1[ch, n, 3] + z1[ch, n, 4]) + (z1[ch, n, 5] + z1[ch, n, 6])
        return own, other

    def step_p(ch):
        if ch == 0:
            wait(lrecv, l_r)
        own, other = sums(ch, S)
        pp[ch, 0] = jnp.exp(own - lrecv[ch])
        pp[ch, 1] = jnp.exp(other - lrecv[ch])

    def gather_z(mine, swapped, dst, ssem, rsem):
        for n, step in enumerate((2, 1, 7)):
            to_zl, to_zh = along(step)
            target = dev(x, to_zl, y, to_zh, c)

            @pl.when(to_zh == zh)
            def _():
                send(mine, dst, ssem.at[n], rsem.at[n], target)

            @pl.when(to_zh != zh)
            def _():
                send(swapped, dst, ssem.at[n], rsem.at[n], target)

    def gather_x(whole, got, ssem, rsem, z_recv):
        for n, step in enumerate((6, 7, 1)):
            wait(got(c, x, along(step)[0]), z_recv.at[n])
        block = whole.at[c, x]
        for n, d in enumerate((2, 1, 3)):
            send(block, block, ssem.at[n], rsem.at[n], dev(rot(x, d, 4), zl, y, zh, c))

    def gather_core(whole, ssem, rsem, x_recv):
        for n, d in enumerate((2, 3, 1)):
            wait(whole.at[c, rot(x, d, 4)], x_recv.at[n])
        send(whole.at[c], whole.at[c], ssem, rsem, core_peer)

    def step_dp(ch):
        for side, place in ((0, agp.at[c, x, zl]), (1, psend)):
            place[0] = jnp.concatenate([pp[0, side], pp[1, side]], axis=0).astype(BF16)
            place[1] = jnp.concatenate([pp[2, side], pp[2, side]], axis=0).astype(BF16)
        gather_z(agp.at[c, x, zl], psend, agp.at[c, x, zl], gp_s.at[0], gp_r.at[0])

    def step_ep(ch):
        gather_x(agp, lambda *at: agp.at[at], gp_s.at[1], gp_r.at[1], gp_r.at[0])

    def step_fp(ch):
        gather_core(agp, gp_s.at[2, 0], gp_r.at[2, 0], gp_r.at[1])

    def step_dd(ch):
        own, other = sums(ch, D)
        p_own, p_other = pp[ch, 0], pp[ch, 1]
        delta = jnp.sum(p_own * own + p_other * other, axis=1, keepdims=True)
        d_own = p_own * (own - delta)
        d_other = p_other * (other - delta)
        place = agd.at[ch, c, x, zl]
        place[...] = jnp.concatenate([d_own, d_other], axis=0).astype(BF16)
        dsend[ch] = jnp.concatenate([d_other, d_own], axis=0).astype(BF16)
        gather_z(place, dsend.at[ch], place, gd_s.at[ch, 0], gd_r.at[ch, 0])

    def step_ed(ch):
        gather_x(
            agd.at[ch], lambda *at: agd.at[(ch, *at)], gd_s.at[ch, 1], gd_r.at[ch, 1], gd_r.at[ch, 0]
        )

    def step_fd(ch):
        gather_core(agd.at[ch], gd_s.at[ch, 2, 0], gd_r.at[ch, 2, 0], gd_r.at[ch, 1])

    down = (((0,), (0,)), ((), ()))
    across = (((1,), (0,)), ((), ()))

    def put(ch, a, value):
        for rp in range(2):
            piece = value[:, rp * 128 : rp * 128 + 128].astype(BF16)
            oo[ch, :, a, rp] = piece.reshape(8, 16, 128)

    def give(ch, part, n):
        for dy, dc in near[1:]:
            yy, cc = rot(y, dy, 4), rot(c, dc, 2)
            send(
                oo.at[ch, yy * 2 + cc, part], orr.at[ch, here, part],
                out_s.at[ch, n], out_r.at[ch, n], dev(x, zl, yy, zh, cc),
            )
        pltpu.make_async_copy(
            oo.at[ch, here, part], orr.at[ch, here, part], out_r.at[ch, n]
        ).start()

    def step_gp(ch):
        if ch == 0:
            wait(agp.at[1 - c], gp_r.at[2, 0])
        tile = agp[:, :, :, ch // 2].reshape(32, 16, 128).astype(F32)
        start = 8 * (ch % 2)
        weights = tile[:, start : start + 8].reshape(256, 128).astype(BF16)
        put(ch, 2, lax.dot_general(weights, both(ch, G), down, preferred_element_type=F32))
        give(ch, pl.ds(2, 1), 0)

    def step_gd(ch):
        wait(agd.at[ch, 1 - c], gd_r.at[ch, 2, 0])
        tile = agd[ch].reshape(32, 16, 128).astype(F32)
        slopes = tile[:, :8].reshape(256, 128).astype(BF16)
        put(ch, 1, lax.dot_general(slopes, both(ch, Q), down, preferred_element_type=F32))
        wait(rc.at[ch, 1 - zh, :, pl.ds(K, 1)], in_r.at[ch, 4])
        mine = agd[ch, zh].reshape(16, 16, 128).astype(F32)
        own = mine[:, :8].reshape(128, 128).astype(BF16)
        other = mine[:, 8:].reshape(128, 128).astype(BF16)
        dq = lax.dot_general(own, half(ch, zh, K), across, preferred_element_type=F32)
        dq += lax.dot_general(other, half(ch, 1 - zh, K), across, preferred_element_type=F32)
        put(ch, 0, dq)
        give(ch, pl.ds(0, 2), 1)

    def step_hp(ch):
        for n in range(CH):
            wait(orr.at[n, :, pl.ds(2, 1)], out_r.at[n, 0])

    def step_hd(ch):
        for n in range(CH):
            wait(orr.at[n, :, pl.ds(0, 2)], out_r.at[n, 1])

    steps = {
        "I": step_i, "J": step_j, "K": step_k, "L": step_l,
        "As": lambda ch: step_a(ch, S), "Ad": lambda ch: step_a(ch, D),
        "Bs": lambda ch: step_b(ch, S),
        "Cs": lambda ch: step_c(ch, S), "Cd": lambda ch: step_c(ch, D),
        "Ds": step_p, "Dp": step_dp, "Ep": step_ep, "Fp": step_fp, "Gp": step_gp, "Hp": step_hp,
        "Dd": step_dd, "Ed": step_ed, "Fd": step_fd, "Gd": step_gd, "Hd": step_hd,
    }
    for name in ORDER:
        steps[name[:-1]](int(name[-1]))

    wait(lsend, l_s)
    wait(agp.at[c], gp_s.at[2, 0])
    for n in range(3):
        wait(agp.at[c, x, zl], gp_s.at[0, n])
        wait(agp.at[c, x], gp_s.at[1, n])
    for ch in range(CH):
        for a, n in ((Q, 0), (G, 2), (K, 4)):
            wait(st.at[ch, :, pl.ds(a, 1)], in_s.at[ch, n])
        for a, n in ((Q, 1), (G, 3)):
            wait(st.at[ch, pl.ds(0, 7), pl.ds(a, 2)], in_s.at[ch, n])
        wait(c1.at[ch], core_s.at[ch])
        wait(x1.at[ch], x_s.at[ch, S])
        wait(xb.at[ch], x_s.at[ch, D])
        for n in range(2):
            wait(z1.at[ch, n], z_s.at[ch, n])
        for n in range(3):
            wait(agd.at[ch, c, x, zl], gd_s.at[ch, 0, n])
            wait(agd.at[ch, c, x], gd_s.at[ch, 1, n])
        wait(agd.at[ch, c], gd_s.at[ch, 2, 0])
        wait(oo.at[ch, pl.ds(0, 7), pl.ds(2, 1)], out_s.at[ch, 0])
        wait(oo.at[ch, pl.ds(0, 7), pl.ds(0, 2)], out_s.at[ch, 1])


def unpack(packed, dq_hbm, dk_hbm, dv_hbm, got, done, load_s, store_s):
    out = (dq_hbm, dk_hbm, dv_hbm)
    loads = [pltpu.make_async_copy(packed.at[:, :, a], got.at[a], load_s.at[a]) for a in range(3)]
    stores = [pltpu.make_async_copy(done.at[a], out[a], store_s.at[a]) for a in range(3)]
    for load in loads:
        load.start()
    for a in range(3):
        loads[a].wait()
        for tile in range(6):
            pair = []
            for head in (2 * tile, 2 * tile + 1):
                yy, ch = head // CH, head % CH
                pair.append(got[a, ch, pl.ds(yy * 2, 2)].reshape(4, 16, 128))
            first, second = swap_halves(*pair)
            lanes = pl.ds(tile * 128, 128)
            for n in range(4):
                done[a, 2 * n, :, lanes] = first[n]
                done[a, 2 * n + 1, :, lanes] = second[n]
        stores[a].start()
    for store in stores:
        store.wait()


def body(query_proj, key_proj, value_proj, grad_output, log_totals):
    dma = pltpu.SemaphoreType.DMA
    anywhere = pl.BlockSpec(memory_space=pl.ANY)
    packed = pl.pallas_call(
        kernel,
        out_shape=jax.ShapeDtypeStruct((CH, 8, 3, 2, 16, 128), BF16),
        in_specs=[anywhere] * 5,
        out_specs=anywhere,
        scratch_shapes=[
            *[pltpu.VMEM(query_proj.shape, BF16)] * 4,
            pltpu.VMEM(log_totals.shape, F32),
            dma((5,)),
            pltpu.VMEM((CH, 8, 4, 2, 16, 128), BF16),
            pltpu.VMEM((CH, 2, 8, 4, 2, 16, 128), BF16),
            pltpu.VMEM((CH, 2, 32, 8, 128), F32),
            pltpu.VMEM((CH, 8, 32, 128), BF16),
            pltpu.VMEM((CH, 7, 32, 128), BF16),
            pltpu.VMEM((CH, 16, 8, 128), F32),
            pltpu.VMEM((CH, 4, 4, 8, 128), F32),
            pltpu.VMEM((CH, 3, 4, 8, 128), F32),
            pltpu.VMEM((CH, 2, 4, 8, 128), F32),
            pltpu.VMEM((CH, 2, 7, 8, 128), F32),
            pltpu.VMEM((CH, 2, 8, 128), F32),
            pltpu.VMEM((2, 4, 4, 2, 16, 128), BF16),
            pltpu.VMEM((2, 16, 128), BF16),
            pltpu.VMEM((CH, 2, 4, 4, 16, 128), BF16),
            pltpu.VMEM((CH, 16, 128), BF16),
            pltpu.VMEM((CH, 8, 3, 2, 16, 128), BF16),
            pltpu.VMEM((CH, 8, 128), F32),
            pltpu.VMEM((CH, 8, 128), F32),
            dma((CH, 5)), dma((CH, 5)),
            dma((CH,)), dma((CH,)),
            dma((CH, 2)), dma((CH, 2)),
            dma((CH, 2)), dma((CH, 2)),
            dma((3, 3)), dma((3, 3)),
            dma((CH, 3, 3)), dma((CH, 3, 3)),
            dma((CH, 2)), dma((CH, 2)),
            dma, dma,
        ],
        compiler_params=pltpu.CompilerParams(
            collective_id=0, has_side_effects=True, vmem_limit_bytes=60 * 2**20
        ),
        name="tied_row_backward",
    )(query_proj, key_proj, value_proj, grad_output, log_totals)
    return pl.pallas_call(
        unpack,
        out_shape=[jax.ShapeDtypeStruct(query_proj.shape, BF16)] * 3,
        in_specs=[anywhere],
        out_specs=[anywhere] * 3,
        scratch_shapes=[
            pltpu.VMEM((3, CH, 8, 2, 16, 128), BF16),
            pltpu.VMEM((3, *query_proj.shape), BF16),
            dma((3,)), dma((3,)),
        ],
        compiler_params=pltpu.CompilerParams(vmem_limit_bytes=60 * 2**20),
        name="unpack_gradients",
    )(packed)


def solution(mesh):
    in_specs = (
        P("row", "col", None),
        P("row", "col", None),
        P("row", "col", None),
        P("row", "col", None),
        P(None, "col"),
    )
    out_specs = (P("row", "col", None), P("row", "col", None), P("row", "col", None))
    return jax.shard_map(body, mesh=mesh, in_specs=in_specs, out_specs=out_specs, check_vma=False)
```
